512 devices in a mesh: ma: 16 (over z_lo, y), an: 8 (over x, core), ka: 4 (over z_hi).
Axes of the slice: x: 4, y: 4, z: 16 (z_hi: 4, z_lo: 4; z = z_hi * 4 + z_lo), core: 2. Of those that a mesh axis runs over, the one named last changes fastest.
Arguments:
- left_matrix: bfloat16 [16384, 4, 1664], P(('ma', 'an'), 'ka'), may hold values from -6 to 6
- right_matrix: bfloat16 [4, 1664, 16384], P('ka', 'ma', 'an'), may hold values from -0.078125 to 0.078125
Outputs:
- product: float32 [16384, 16384], P(('ma', 'ka'), 'an')
The draws below stay inside these ranges and needn't reach their ends.
All inputs are finite; a program needn't handle non-finite values.
Results may differ from the reference program's by a relative error of at most 0.012.
Values may be sent and summed in bfloat16 or wider, within the bound.
A program may use at most 64 MiB of HBM per device.

```python
import jax
import jax.numpy as jnp
from jax import lax

M = 16384
N = 16384
KB = 4
KW = 1664
K = 6656
N_KA = 4


def shard_levels(stream_key, shape, pieces, least, top_value):
    loudness = 1.0
    for position, shards_of in pieces:
        steps = jax.random.uniform(jax.random.fold_in(jax.random.fold_in(stream_key, 6), position), (shards_of,), jnp.float32, least / len(pieces), top_value / len(pieces))
        loudness = loudness * jnp.repeat(jnp.exp(steps), shape[position] // shards_of).reshape((-1,) + (1,) * (len(shape) - 1 - position))
    return loudness


def normal_values(rng, shape, deviation, limit, cuts=(), dtype=jnp.bfloat16):
    array = jax.random.normal(rng, shape, jnp.float32) * deviation
    if len(cuts) > 0:
        array = shard_levels(rng, shape, cuts, -0.22, 0.18) * array
    return jnp.clip(array, min=-limit, max=limit).astype(dtype)


def setup_inputs(seed: int = 0) -> dict:
    key_list = jax.random.split(jax.random.key(seed), 3)
    return {
        "left_matrix": normal_values(key_list[0], (M, KB, KW), 1.0, 6.0, ((0, 128), (1, 4))),
        "right_matrix": normal_values(key_list[1], (KB, KW, N), K ** -0.5, 0.078125, ((0, 4), (1, 16), (2, 8))),
    }


def reference(left_matrix, right_matrix):
    product = jnp.zeros((M, N), jnp.float32)
    for slab_index in range(N_KA):
        partial_sum = jnp.dot(left_matrix[:, slab_index, :], right_matrix[slab_index], preferred_element_type=jnp.float32)
        rounded = lax.optimization_barrier(partial_sum.astype(jnp.bfloat16))
        product = product + rounded.astype(jnp.float32)
    return product
```

```python
import jax
import jax.numpy as jnp
from jax import lax
from jax.experimental import pallas as pl
from jax.experimental.pallas import tpu as pltpu
from jax.sharding import PartitionSpec as P

MESH = pl.DeviceIdType.MESH
CHUNKS, WIDTH = 2, 256


def kernel(left, right, out, hop, rows, stage, cols, total, give, take, local,
           xs_s, xs_r, zm_s, zm_r, p1_s, p1_r, p2_s, p2_r, co_s, co_r, ra_s, ra_r, ri_s, ri_r, ou_s, ou_r):
    ma, an, hi = lax.axis_index("ma"), lax.axis_index("an"), lax.axis_index("ka")
    lo, y = ma // 4, lax.rem(ma, 4)
    x, c = an // 2, lax.rem(an, 2)
    z = hi * 4 + lo

    def turn(i, d, n=4):
        return lax.rem(i + d + n, n)

    def to_x(d):
        return {"an": turn(x, d) * 2 + c}

    def to_y(d):
        return {"ma": lo * 4 + turn(y, d)}

    def to_z(d):
        level = turn(z, d, 16)
        return {"ma": lax.rem(level, 4) * 4 + y, "ka": level // 4}

    def to_hi(d):
        return {"ka": turn(hi, d)}

    to_core = {"an": x * 2 + 1 - c}

    def remote(src, dst, send, recv, device):
        return pltpu.make_async_remote_copy(
            src_ref=src, dst_ref=dst, send_sem=send, recv_sem=recv, device_id=device, device_id_type=MESH
        )

    barrier = pltpu.get_barrier_semaphore()
    friends = [to(d) for to in (to_x, to_y, to_hi) for d in (1, 2, 3)] + [to_z(1), to_z(-1), to_core]
    for friend in friends:
        pl.semaphore_signal(barrier, inc=1, device_id=friend, device_id_type=MESH)
    pl.semaphore_wait(barrier, len(friends))

    sent = []

    def send(*args):
        copy = remote(*args)
        copy.start()
        sent.append(copy)

    def await_into(dst, sem):
        remote(dst, dst, sem, sem, to_core).wait_recv()

    for d in (2, 1, 3):
        send(left.at[:, turn(x, d)], hop.at[x], xs_s.at[d - 1], xs_r.at[d - 1], to_x(d))
    own_hop = pltpu.make_async_copy(left.at[:, x], hop.at[x], local.at[0])
    own_hop.start()
    own_stage = []
    for ch in range(CHUNKS):
        for d in (2, 1, 3):
            at = pl.ds(pl.multiple_of(turn(y, d) * (CHUNKS * WIDTH) + ch * WIDTH, WIDTH), WIDTH)
            i = ch * 3 + d - 1
            send(right.at[:, at], stage.at[ch, y], ra_s.at[i], ra_r.at[i], to_y(d))
        at = pl.ds(pl.multiple_of(y * (CHUNKS * WIDTH) + ch * WIDTH, WIDTH), WIDTH)
        own_stage.append(pltpu.make_async_copy(right.at[:, at], stage.at[ch, y], local.at[1 + ch]))
        own_stage[-1].start()

    own_hop.wait()
    for d in (1, 2, 3):
        await_into(hop.at[turn(x, -d)], xs_r.at[d - 1])
    for d in (2, 1, 3):
        send(hop.at[turn(hi, d)], rows.at[hi, y, c, :, x], zm_s.at[d - 1], zm_r.at[d - 1], to_hi(d))
    own_rows = pltpu.make_async_copy(hop.at[hi], rows.at[hi, y, c, :, x], local.at[3])
    own_rows.start()

    def settle(ch):
        own_stage[ch].wait()
        for d in (1, 2, 3):
            await_into(stage.at[ch, turn(y, -d)], ra_r.at[ch * 3 + d - 1])
        block = stage[ch].astype(jnp.float32).reshape(cols.shape[2] * cols.shape[3], WIDTH)
        cols[ch, z] = block.astype(jnp.bfloat16).reshape(cols.shape[2:])

    def ring_index(ch, s, way, sub):
        return ((ch * 8 + s - 1) * 2 + way) * 2 + sub

    def ring(ch, s):
        for sub in (0, 1):
            for way, sign in ((0, 1), (1, -1)):
                block = cols.at[ch, turn(z, -sign * (s - 1), 16), sub]
                if s > 1:
                    await_into(block, ri_r.at[ring_index(ch, s - 1, way, sub)])
                if s == 8 and sub != way:
                    continue
                i = ring_index(ch, s, way, sub)
                send(block, block, ri_s.at[i], ri_r.at[i], to_z(sign))

    def ring_end(ch):
        for way in (0, 1):
            await_into(cols.at[ch, turn(z, 8, 16), way], ri_r.at[ring_index(ch, 8, way, way)])

    def gather_one():
        own_rows.wait()
        for d in (1, 2, 3):
            await_into(rows.at[turn(hi, -d), y, c, :, x], zm_r.at[d - 1])
        for d in (2, 1, 3):
            mine = rows.at[:, y, c, 0, x]
            send(mine, mine, p1_s.at[d - 1], p1_r.at[d - 1], to_x(d))
            mine = rows.at[:, y, c, 1, x]
            send(mine, mine, p1_s.at[d + 2], p1_r.at[d + 2], to_y(d))

    def gather_two():
        for d in (1, 2, 3):
            await_into(rows.at[:, y, c, 0, turn(x, -d)], p1_r.at[d - 1])
            await_into(rows.at[:, turn(y, -d), c, 1, x], p1_r.at[d + 2])
        for k in range(4):
            for d in (2, 1, 3):
                i = (k * 3 + d - 1) * 2
                mine = rows.at[turn(hi, k), y, c, 0]
                send(mine, mine, p2_s.at[i], p2_r.at[i], to_y(d))
                mine = rows.at[turn(hi, k), :, c, 1, x]
                send(mine, mine, p2_s.at[i + 1], p2_r.at[i + 1], to_x(d))
        mine = rows.at[:, y, c, 0]
        send(mine, mine, co_s.at[24], co_r.at[24], to_core)
        mine = rows.at[:, :, c, 1, x]
        send(mine, mine, co_s.at[25], co_r.at[25], to_core)

    def pass_on(k):
        for d in (1, 3, 2):
            i = (k * 3 + d - 1) * 2
            got = rows.at[turn(hi, k), turn(y, -d), c, 0]
            await_into(got, p2_r.at[i])
            send(got, got, co_s.at[i], co_r.at[i], to_core)
            got = rows.at[turn(hi, k), :, c, 1, turn(x, -d)]
            await_into(got, p2_r.at[i + 1])
            send(got, got, co_s.at[i + 1], co_r.at[i + 1], to_core)

    def get_rest(k):
        if k == 0:
            await_into(rows.at[:, y, 1 - c, 0], co_r.at[24])
            await_into(rows.at[:, :, 1 - c, 1, x], co_r.at[25])
        for d in (1, 3, 2):
            i = (k * 3 + d - 1) * 2
            await_into(rows.at[turn(hi, k), turn(y, -d), 1 - c, 0], co_r.at[i])
            await_into(rows.at[turn(hi, k), :, 1 - c, 1, turn(x, -d)], co_r.at[i + 1])

    def multiply(ch, k, first=False):
        block = turn(hi, k)

        def one(i, carry):
            a = rows[block, i].reshape(256, rows.shape[-1])
            b = cols[ch, pl.ds(block * 4, 4)].reshape(rows.shape[-1], WIDTH)
            term = jnp.dot(a, b, preferred_element_type=jnp.float32)
            total[ch, i] = term if first else total[ch, i] + term
            return carry

        lax.fori_loop(0, 4, one, 0)

    def hand_out(ch):
        give[ch] = total[ch].astype(jnp.bfloat16)
        for d in (2, 1, 3):
            i = ch * 3 + d - 1
            send(give.at[ch, turn(y, d)], take.at[ch, y], ou_s.at[i], ou_r.at[i], to_y(d))
        own = pltpu.make_async_copy(give.at[ch, y], take.at[ch, y], local.at[4 + ch])
        own.start()
        return own

    def collect(ch, own):
        own.wait()
        for d in (1, 2, 3):
            await_into(take.at[ch, turn(y, -d)], ou_r.at[ch * 3 + d - 1])
        for i in range(4):
            out[:, pl.ds((i * CHUNKS + ch) * WIDTH, WIDTH)] = take[ch, i]

    settle(0)
    ring(0, 1)
    settle(1)
    ring(0, 2)
    ring(0, 3)
    gather_one()
    ring(0, 4)
    ring(0, 5)
    ring(0, 6)
    gather_two()
    ring(0, 7)
    ring(0, 8)
    ring(1, 1)
    ring(1, 2)
    pass_on(0)
    ring(1, 3)
    pass_on(1)
    ring(1, 4)
    pass_on(2)
    ring(1, 5)
    pass_on(3)
    ring(1, 6)
    ring_end(0)
    get_rest(0)
    multiply(0, 0, first=True)
    get_rest(1)
    multiply(0, 1)
    ring(1, 7)
    get_rest(2)
    multiply(0, 2)
    get_rest(3)
    multiply(0, 3)
    ring(1, 8)
    own0 = hand_out(0)
    for k in (0, 1, 3):
        multiply(1, k, first=k == 0)
    collect(0, own0)
    ring_end(1)
    multiply(1, 2)
    own1 = hand_out(1)
    collect(1, own1)
    for copy in sent:
        copy.wait_send()


def per_device(left_matrix, right_matrix):
    depth = left_matrix.shape[2]
    left = left_matrix.reshape(2, 4, 16, depth)
    right = right_matrix.reshape(right_matrix.shape[1:])
    dma = pltpu.SemaphoreType.DMA
    counts = (3, 3, 6, 24, 26, 6, CHUNKS * 32, 6)
    product = pl.pallas_call(
        kernel,
        out_shape=jax.ShapeDtypeStruct((256, right.shape[1]), jnp.bfloat16),
        in_specs=[pl.BlockSpec(memory_space=pl.ANY)] * 2,
        out_specs=pl.BlockSpec(memory_space=pltpu.VMEM),
        scratch_shapes=[
            pltpu.VMEM((4, 2, 16, depth), jnp.bfloat16),
            pltpu.VMEM((4, 4, 2, 2, 4, 16, depth), jnp.bfloat16),
            pltpu.VMEM((CHUNKS, 4, right.shape[0], WIDTH), jnp.bfloat16),
            pltpu.VMEM((CHUNKS, 16, 2, right.shape[0] * 2, WIDTH), jnp.bfloat16),
            pltpu.VMEM((CHUNKS, 4, 256, WIDTH), jnp.float32),
            pltpu.VMEM((CHUNKS, 4, 256, WIDTH), jnp.bfloat16),
            pltpu.VMEM((CHUNKS, 4, 256, WIDTH), jnp.bfloat16),
            dma((6,)),
        ]
        + [dma((n,)) for n in counts for _ in range(2)],
        compiler_params=pltpu.CompilerParams(
            collective_id=0, has_side_effects=True, vmem_limit_bytes=56 * 2**20
        ),
    )(left, right)
    return product.astype(jnp.float32)


def solution(mesh):
    in_specs = (P(("ma", "an"), "ka", None), P("ka", "ma", "an"))
    out_specs = P(("ma", "ka"), "an")
    return jax.shard_map(per_device, mesh=mesh, in_specs=in_specs, out_specs=out_specs, check_vma=False)
```

```python
import jax
import jax.numpy as jnp
from jax import lax
from jax.experimental import pallas as pl
from jax.experimental.pallas import tpu as pltpu
from jax.sharding import PartitionSpec as P

MESH = pl.DeviceIdType.MESH
WIDTHS = (256, 256)
STARTS = tuple(sum(WIDTHS[:ch]) for ch in range(len(WIDTHS)))
QUARTER = sum(WIDTHS)
CHUNKS = len(WIDTHS)


def kernel(left, right, out, hop, relay, rows, *refs):
    refs = list(refs)

    def take_refs(n):
        taken, refs[:n] = refs[:n], []
        return taken

    stage, cols, total, give, take = (take_refs(CHUNKS) for _ in range(5))
    up, down, local, xs_s, xs_r, zm_s, zm_r, p1_s, p1_r, p2_s, p2_r, co_s, co_r, ra_s, ra_r, ri_s, ri_r, ou_s, ou_r = refs
    depth = rows.shape[-1]
    ma, an, hi = lax.axis_index("ma"), lax.axis_index("an"), lax.axis_index("ka")
    lo, y = ma // 4, lax.rem(ma, 4)
    x, c = an // 2, lax.rem(an, 2)
    z = hi * 4 + lo

    def turn(i, d, n=4):
        return lax.rem(i + d + n, n)

    def to_x(d):
        return {"an": turn(x, d) * 2 + c}

    def to_y(d):
        return {"ma": lo * 4 + turn(y, d)}

    def to_z(d):
        level = turn(z, d, 16)
        return {"ma": lax.rem(level, 4) * 4 + y, "ka": level // 4}

    def to_hi(d):
        return {"ka": turn(hi, d)}

    to_core = {"an": x * 2 + 1 - c}

    def remote(src, dst, send, recv, device):
        return pltpu.make_async_remote_copy(
            src_ref=src, dst_ref=dst, send_sem=send, recv_sem=recv, device_id=device, device_id_type=MESH
        )

    barrier = pltpu.get_barrier_semaphore()
    friends = [to(d) for to in (to_x, to_y) for d in (1, 2, 3)] + [to_z(-1), to_core]
    for friend in friends:
        pl.semaphore_signal(barrier, inc=1, device_id=friend, device_id_type=MESH)
    pl.semaphore_wait(barrier, len(friends))

    sent = []

    def send(*args):
        copy = remote(*args)
        copy.start()
        sent.append(copy)

    def await_into(dst, sem):
        remote(dst, dst, sem, sem, to_core).wait_recv()

    def hear(r):
        if r >= 2:
            pl.semaphore_wait(down.at[r - 1], 1)
        if r >= 3:
            pl.semaphore_wait(up.at[r - 1], 1)
        if r <= 4:
            pl.semaphore_signal(down.at[r], inc=1, device_id=to_z(1), device_id_type=MESH)
        if 2 <= r <= 4:
            pl.semaphore_signal(up.at[r], inc=1, device_id=to_z(-1), device_id_type=MESH)

    own = {}

    def start_local(src, dst, i):
        own[i] = pltpu.make_async_copy(src, dst, local.at[i])
        own[i].start()

    def columns(ch, of):
        return pl.ds(pl.multiple_of(of * QUARTER + STARTS[ch], 128), WIDTHS[ch])

    def scatter():
        for d in (2, 1, 3):
            send(left.at[:, turn(x, d)], hop.at[x], xs_s.at[d - 1], xs_r.at[d - 1], to_x(d))
        start_local(left.at[:, x], hop.at[x], 0)

    def spread(ch):
        for d in (2, 1, 3):
            i = ch * 3 + d - 1
            send(right.at[:, columns(ch, turn(y, d))], stage[ch].at[y], ra_s.at[i], ra_r.at[i], to_y(d))
        start_local(right.at[:, columns(ch, y)], stage[ch].at[y], 2 + ch)

    def settle(ch):
        own[2 + ch].wait()
        for d in (1, 2, 3):
            await_into(stage[ch].at[turn(y, -d)], ra_r.at[ch * 3 + d - 1])
        block = stage[ch][...].astype(jnp.float32).reshape(-1, WIDTHS[ch])
        cols[ch][z] = block.astype(jnp.bfloat16).reshape(cols[ch].shape[1:])

    def scattered():
        own[0].wait()
        for d in (1, 2, 3):
            await_into(hop.at[turn(x, -d)], xs_r.at[d - 1])
        start_local(hop.at[hi], rows.at[hi, y, c, :, x], 1)

    def lift(d):
        if d == 2:
            for half, way in ((0, 1), (1, 3)):
                send(hop.at[turn(hi, 2), half], relay.at[half], zm_s.at[half], zm_r.at[half], to_hi(way))
        else:
            send(hop.at[turn(hi, d)], rows.at[hi, y, c, :, x], zm_s.at[1 + d], zm_r.at[1 + d], to_hi(d))

    def lift_on():
        for half, way in ((0, 1), (1, 3)):
            await_into(relay.at[half], zm_r.at[half])
            i = 3 + 2 * half
            send(relay.at[half], rows.at[turn(hi, -way), y, c, half, x], zm_s.at[i], zm_r.at[i], to_hi(way))

    def ring_index(ch, s, way, sub):
        return ((ch * 8 + s - 1) * 2 + way) * 2 + sub

    def ring(ch, s, ways=(0, 1)):
        for sub in (0, 1):
            for way in ways:
                sign = 1 - 2 * way
                block = cols[ch].at[turn(z, -sign * (s - 1), 16), sub]
                if s > 1:
                    await_into(block, ri_r.at[ring_index(ch, s - 1, way, sub)])
                if s == 8 and sub != way:
                    continue
                i = ring_index(ch, s, way, sub)
                send(block, block, ri_s.at[i], ri_r.at[i], to_z(sign))

    def ring_end(ch):
        for way in (0, 1):
            await_into(cols[ch].at[turn(z, 8, 16), way], ri_r.at[ring_index(ch, 8, way, way)])

    def gather_one(k):
        block = turn(hi, k)
        if k == 0:
            own[1].wait()
        else:
            if k == 2:
                for half in (0, 1):
                    await_into(rows.at[block, y, c, half, x], zm_r.at[3 + 2 * half])
            else:
                await_into(rows.at[block, y, c, :, x], zm_r.at[5 - k])
        for d in (2, 1, 3):
            i = (k * 3 + d - 1) * 2
            for half, to in ((0, to_x(d)), (1, to_y(d))):
                mine = rows.at[block, y, c, half, x]
                send(mine, mine, p1_s.at[i + half], p1_r.at[i + half], to)

    def gather_two(k):
        block = turn(hi, k)
        for d in (1, 3, 2):
            i = (k * 3 + d - 1) * 2
            await_into(rows.at[block, y, c, 0, turn(x, -d)], p1_r.at[i])
            await_into(rows.at[block, turn(y, -d), c, 1, x], p1_r.at[i + 1])
        for d in (2, 1, 3, 0):
            for half, mine in ((0, rows.at[block, y, c, 0]), (1, rows.at[block, :, c, 1, x])):
                if d == 0:
                    i = k * 8 + half
                    send(mine, mine, co_s.at[i], co_r.at[i], to_core)
                else:
                    i = (k * 3 + d - 1) * 2 + half
                    send(mine, mine, p2_s.at[i], p2_r.at[i], to_x(d) if half else to_y(d))

    def pass_on(k):
        block = turn(hi, k)
        for d in (1, 3, 2):
            i, j = (k * 3 + d - 1) * 2, k * 8 + 2 * d
            for half, got in ((0, rows.at[block, turn(y, -d), c, 0]), (1, rows.at[block, :, c, 1, turn(x, -d)])):
                await_into(got, p2_r.at[i + half])
                send(got, got, co_s.at[j + half], co_r.at[j + half], to_core)

    def get_rest(k):
        block = turn(hi, k)
        for d in (0, 1, 3, 2):
            j = k * 8 + 2 * d
            await_into(rows.at[block, turn(y, -d), 1 - c, 0], co_r.at[j])
            await_into(rows.at[block, :, 1 - c, 1, turn(x, -d)], co_r.at[j + 1])

    begun = set()

    def multiply(ch, k):
        block, first = turn(hi, k), ch not in begun
        begun.add(ch)

        a = rows[block].reshape(-1, depth)
        b = cols[ch][pl.ds(block * 4, 4)].reshape(depth, WIDTHS[ch])
        term = jnp.dot(a, b, preferred_element_type=jnp.float32)
        total[ch][...] = term if first else total[ch][...] + term

    def hand_out(ch, k):
        block = turn(hi, k)
        for d in (2, 1, 3, 0):
            of = turn(y, d)
            at = pl.ds(pl.multiple_of(of * 256, 256), 256)
            a = rows[block, of].reshape(256, depth)
            b = cols[ch][pl.ds(block * 4, 4)].reshape(depth, WIDTHS[ch])
            term = jnp.dot(a, b, preferred_element_type=jnp.float32)
            give[ch][of] = (total[ch][at] + term).astype(jnp.bfloat16)
            if d:
                i = ch * 3 + d - 1
                send(give[ch].at[of], take[ch].at[y], ou_s.at[i], ou_r.at[i], to_y(d))
        start_local(give[ch].at[y], take[ch].at[y], 2 + CHUNKS + ch)

    def collect(ch):
        own[2 + CHUNKS + ch].wait()
        for d in (1, 2, 3):
            await_into(take[ch].at[turn(y, -d)], ou_r.at[ch * 3 + d - 1])
        for i in range(4):
            out[:, pl.ds(i * QUARTER + STARTS[ch], WIDTHS[ch])] = take[ch][i]

    hear(1)
    spread(0)
    scatter()
    spread(1)
    settle(0)
    ring(0, 1, (0,))
    hear(2)
    ring(0, 1, (1,))
    settle(1)
    scattered()
    gather_one(0)
    hear(3)
    hear(4)
    hear(5)
    lift(1)
    lift(3)
    lift(2)
    ring(0, 2)
    gather_two(0)
    ring(0, 3)
    ring(0, 4)
    lift_on()
    ring(1, 1)
    gather_one(1)
    gather_one(3)
    pass_on(0)
    ring(0, 5)
    gather_two(1)
    gather_two(3)
    ring(1, 2)
    gather_one(2)
    ring(0, 6)
    get_rest(0)
    ring(1, 3)
    multiply(0, 0)
    gather_two(2)
    pass_on(1)
    pass_on(3)
    ring(0, 7)
    get_rest(1)
    get_rest(3)
    ring(1, 4)
    ring(0, 8)
    pass_on(2)
    multiply(0, 1)
    multiply(0, 3)
    get_rest(2)
    ring(1, 5)
    ring_end(0)
    hand_out(0, 2)
    ring(1, 6)
    multiply(1, 0)
    ring(1, 7)
    collect(0)
    ring(1, 8)
    multiply(1, 1)
    multiply(1, 3)
    ring_end(1)
    hand_out(1, 2)
    collect(1)
    for copy in sent:
        copy.wait_send()


def per_device(left_matrix, right_matrix):
    depth, strip = left_matrix.shape[2], right_matrix.shape[1]
    left = left_matrix.reshape(2, 4, 16, depth)
    right = right_matrix.reshape(right_matrix.shape[1:])
    dma, regular = pltpu.SemaphoreType.DMA, pltpu.SemaphoreType.REGULAR
    counts = (3, 6, 24, 24, 32, CHUNKS * 3, CHUNKS * 32, CHUNKS * 3)
    bf16 = jnp.bfloat16
    product = pl.pallas_call(
        kernel,
        out_shape=pltpu.VMEM((256, right.shape[1]), bf16),
        in_specs=[pl.BlockSpec(memory_space=pl.ANY)] * 2,
        out_specs=pl.BlockSpec(memory_space=pltpu.VMEM),
        scratch_shapes=[
            pltpu.VMEM((4, 2, 16, depth), bf16),
            pltpu.VMEM((2, 16, depth), bf16),
            pltpu.VMEM((4, 4, 2, 2, 4, 16, depth), bf16),
            *[pltpu.VMEM((4, strip, width), bf16) for width in WIDTHS],
            *[pltpu.VMEM((16, 2, strip * 2, width), bf16) for width in WIDTHS],
            *[pltpu.VMEM((1024, width), jnp.float32) for width in WIDTHS],
            *[pltpu.VMEM((4, 256, width), bf16) for width in WIDTHS * 2],
            regular((5,)),
            regular((5,)),
            dma((2 + 2 * CHUNKS,)),
            *[dma((n,)) for n in counts for _ in range(2)],
        ],
        compiler_params=pltpu.CompilerParams(
            collective_id=0, has_side_effects=True, vmem_limit_bytes=56 * 2**20
        ),
    )(left, right)
    return product.astype(jnp.float32)


def solution(mesh):
    in_specs = (P(("ma", "an"), "ka", None), P("ka", "ma", "an"))
    out_specs = P(("ma", "ka"), "an")
    return jax.shard_map(per_device, mesh=mesh, in_specs=in_specs, out_specs=out_specs, check_vma=False)
```

```python
import jax
import jax.numpy as jnp
from jax import lax
from jax.experimental import pallas as pl
from jax.experimental.pallas import tpu as pltpu
from jax.sharding import PartitionSpec as P

MESH = pl.DeviceIdType.MESH
WIDTHS = (256, 256)
STARTS = tuple(sum(WIDTHS[:ch]) for ch in range(len(WIDTHS)))
QUARTER = sum(WIDTHS)
CHUNKS = len(WIDTHS)


def kernel(left, right, out, hop, relay, rows, *refs):
    refs = list(refs)

    def take_refs(n):
        taken, refs[:n] = refs[:n], []
        return taken

    stage, cols, total, give, take = (take_refs(CHUNKS) for _ in range(5))
    up, down, local, xs_s, xs_r, zm_s, zm_r, p1_s, p1_r, p2_s, p2_r, co_s, co_r, ra_s, ra_r, ri_s, ri_r, ou_s, ou_r = refs
    depth = rows.shape[-1]
    ma, an, hi = lax.axis_index("ma"), lax.axis_index("an"), lax.axis_index("ka")
    lo, y = ma // 4, lax.rem(ma, 4)
    x, c = an // 2, lax.rem(an, 2)
    z = hi * 4 + lo

    def turn(i, d, n=4):
        return lax.rem(i + d + n, n)

    def to_x(d):
        return {"an": turn(x, d) * 2 + c}

    def to_y(d):
        return {"ma": lo * 4 + turn(y, d)}

    def to_z(d):
        level = turn(z, d, 16)
        return {"ma": lax.rem(level, 4) * 4 + y, "ka": level // 4}

    def to_hi(d):
        return {"ka": turn(hi, d)}

    to_core = {"an": x * 2 + 1 - c}

    def remote(src, dst, send, recv, device):
        return pltpu.make_async_remote_copy(
            src_ref=src, dst_ref=dst, send_sem=send, recv_sem=recv, device_id=device, device_id_type=MESH
        )

    barrier = pltpu.get_barrier_semaphore()
    friends = [to(d) for to in (to_x, to_y) for d in (1, 2, 3)] + [to_z(-1), to_core]
    for friend in friends:
        pl.semaphore_signal(barrier, inc=1, device_id=friend, device_id_type=MESH)
    pl.semaphore_wait(barrier, len(friends))

    sent = []

    def send(*args):
        copy = remote(*args)
        copy.start()
        sent.append(copy)

    def flush(keep):
        while len(sent) > keep:
            sent.pop(0).wait_send()

    def await_into(dst, sem):
        remote(dst, dst, sem, sem, to_core).wait_recv()

    def hear(r):
        if r >= 2:
            pl.semaphore_wait(down.at[r - 1], 1)
        if r >= 3:
            pl.semaphore_wait(up.at[r - 1], 1)
        if r <= 4:
            pl.semaphore_signal(down.at[r], inc=1, device_id=to_z(1), device_id_type=MESH)
        if 2 <= r <= 4:
            pl.semaphore_signal(up.at[r], inc=1, device_id=to_z(-1), device_id_type=MESH)

    own = {}

    def start_local(src, dst, i):
        own[i] = pltpu.make_async_copy(src, dst, local.at[i])
        own[i].start()

    def columns(ch, of):
        return pl.ds(pl.multiple_of(of * QUARTER + STARTS[ch], 128), WIDTHS[ch])

    def scatter():
        for d in (2, 1, 3):
            send(left.at[:, turn(x, d)], hop.at[x], xs_s.at[d - 1], xs_r.at[d - 1], to_x(d))
        start_local(left.at[:, x], hop.at[x], 0)

    def spread(ch):
        for d in (2, 1, 3):
            i = ch * 3 + d - 1
            send(right.at[:, columns(ch, turn(y, d))], stage[ch].at[y], ra_s.at[i], ra_r.at[i], to_y(d))
        start_local(right.at[:, columns(ch, y)], stage[ch].at[y], 2 + ch)

    def settle(ch):
        own[2 + ch].wait()
        for d in (1, 2, 3):
            await_into(stage[ch].at[turn(y, -d)], ra_r.at[ch * 3 + d - 1])
        block = stage[ch][...].astype(jnp.float32).reshape(-1, WIDTHS[ch])
        cols[ch][z] = block.astype(jnp.bfloat16).reshape(cols[ch].shape[1:])

    def scattered():
        own[0].wait()
        for d in (1, 2, 3):
            await_into(hop.at[turn(x, -d)], xs_r.at[d - 1])
        start_local(hop.at[hi], rows.at[hi, y, c, :, x], 1)

    def lift(d):
        if d == 2:
            for half, way in ((0, 1), (1, 3)):
                send(hop.at[turn(hi, 2), half], relay.at[half], zm_s.at[half], zm_r.at[half], to_hi(way))
        else:
            send(hop.at[turn(hi, d)], rows.at[hi, y, c, :, x], zm_s.at[1 + d], zm_r.at[1 + d], to_hi(d))

    def lift_on():
        for half, way in ((0, 1), (1, 3)):
            await_into(relay.at[half], zm_r.at[half])
            i = 3 + 2 * half
            send(relay.at[half], rows.at[turn(hi, -way), y, c, half, x], zm_s.at[i], zm_r.at[i], to_hi(way))

    def ring_index(ch, s, way, sub):
        return ((ch * 8 + s - 1) * 2 + way) * 2 + sub

    def ring(ch, s, ways=(0, 1)):
        for sub in (0, 1):
            for way in ways:
                sign = 1 - 2 * way
                block = cols[ch].at[turn(z, -sign * (s - 1), 16), sub]
                if s > 1:
                    await_into(block, ri_r.at[ring_index(ch, s - 1, way, sub)])
                if s == 8 and sub != way:
                    continue
                i = ring_index(ch, s, way, sub)
                send(block, block, ri_s.at[i], ri_r.at[i], to_z(sign))

    def ring_end(ch):
        for way in (0, 1):
            await_into(cols[ch].at[turn(z, 8, 16), way], ri_r.at[ring_index(ch, 8, way, way)])

    def gather_one(k):
        block = turn(hi, k)
        if k == 0:
            own[1].wait()
        else:
            if k == 2:
                for half in (0, 1):
                    await_into(rows.at[block, y, c, half, x], zm_r.at[3 + 2 * half])
            else:
                await_into(rows.at[block, y, c, :, x], zm_r.at[5 - k])
        for d in (2, 1, 3):
            i = (k * 3 + d - 1) * 2
            for half, to in ((0, to_x(d)), (1, to_y(d))):
                mine = rows.at[block, y, c, half, x]
                send(mine, mine, p1_s.at[i + half], p1_r.at[i + half], to)

    def gather_two(k):
        block = turn(hi, k)
        for d in (1, 3, 2):
            i = (k * 3 + d - 1) * 2
            await_into(rows.at[block, y, c, 0, turn(x, -d)], p1_r.at[i])
            await_into(rows.at[block, turn(y, -d), c, 1, x], p1_r.at[i + 1])
        for d in (2, 1, 3, 0):
            for half, mine in ((0, rows.at[block, y, c, 0]), (1, rows.at[block, :, c, 1, x])):
                if d == 0:
                    i = k * 8 + half
                    send(mine, mine, co_s.at[i], co_r.at[i], to_core)
                else:
                    i = (k * 3 + d - 1) * 2 + half
                    send(mine, mine, p2_s.at[i], p2_r.at[i], to_x(d) if half else to_y(d))

    def pass_on(k):
        block = turn(hi, k)
        for d in (1, 3, 2):
            i, j = (k * 3 + d - 1) * 2, k * 8 + 2 * d
            for half, got in ((0, rows.at[block, turn(y, -d), c, 0]), (1, rows.at[block, :, c, 1, turn(x, -d)])):
                await_into(got, p2_r.at[i + half])
                send(got, got, co_s.at[j + half], co_r.at[j + half], to_core)

    def get_rest(k):
        block = turn(hi, k)
        for d in (0, 1, 3, 2):
            j = k * 8 + 2 * d
            await_into(rows.at[block, turn(y, -d), 1 - c, 0], co_r.at[j])
            await_into(rows.at[block, :, 1 - c, 1, turn(x, -d)], co_r.at[j + 1])

    begun = set()

    def multiply(ch, k):
        block, first = turn(hi, k), ch not in begun
        begun.add(ch)

        a = rows[block].reshape(-1, depth)
        b = cols[ch][pl.ds(block * 4, 4)].reshape(depth, WIDTHS[ch])
        term = jnp.dot(a, b, preferred_element_type=jnp.float32)
        total[ch][...] = term if first else total[ch][...] + term

    def hand_out(ch, k):
        block = turn(hi, k)
        for d in (2, 1, 3, 0):
            of = turn(y, d)
            at = pl.ds(pl.multiple_of(of * 256, 256), 256)
            a = rows[block, of].reshape(256, depth)
            b = cols[ch][pl.ds(block * 4, 4)].reshape(depth, WIDTHS[ch])
            term = jnp.dot(a, b, preferred_element_type=jnp.float32)
            give[ch][of] = (total[ch][at] + term).astype(jnp.bfloat16)
            if d:
                i = ch * 3 + d - 1
                send(give[ch].at[of], take[ch].at[y], ou_s.at[i], ou_r.at[i], to_y(d))
        start_local(give[ch].at[y], take[ch].at[y], 2 + CHUNKS + ch)

    def collect(ch):
        own[2 + CHUNKS + ch].wait()
        for d in (1, 2, 3):
            await_into(take[ch].at[turn(y, -d)], ou_r.at[ch * 3 + d - 1])
        for i in range(4):
            out[:, pl.ds(i * QUARTER + STARTS[ch], WIDTHS[ch])] = take[ch][i]

    hear(1)
    spread(0)
    scatter()
    spread(1)
    settle(0)
    ring(0, 1, ways=(0,))
    hear(2)
    ring(0, 1, ways=(1,))
    settle(1)
    scattered()
    gather_one(0)
    hear(3)
    hear(4)
    hear(5)
    lift(1)
    lift(3)
    lift(2)
    ring(0, 2)
    gather_two(0)
    ring(0, 3)
    ring(1, 1)
    ring(0, 4)
    ring(1, 2)
    lift_on()
    gather_one(1)
    gather_one(3)
    pass_on(0)
    ring(0, 5)
    gather_two(1)
    gather_two(3)
    ring(1, 3)
    gather_one(2)
    ring(0, 6)
    get_rest(0)
    ring(1, 4)
    multiply(0, 0)
    gather_two(2)
    ring(0, 7)
    pass_on(1)
    pass_on(3)
    ring(1, 5)
    get_rest(1)
    get_rest(3)
    ring(0, 8)
    multiply(1, 0)
    multiply(0, 1)
    pass_on(2)
    ring(1, 6)
    multiply(0, 3)
    get_rest(2)
    ring_end(0)
    hand_out(0, 2)
    ring(1, 7)
    collect(0)
    ring(1, 8)
    multiply(1, 1)
    multiply(1, 3)
    ring_end(1)
    hand_out(1, 2)
    flush(3)
    collect(1)
    flush(0)


def per_device(left_matrix, right_matrix):
    depth, strip = left_matrix.shape[2], right_matrix.shape[1]
    left = left_matrix.reshape(2, 4, 16, depth)
    right = right_matrix.reshape(right_matrix.shape[1:])
    dma, regular = pltpu.SemaphoreType.DMA, pltpu.SemaphoreType.REGULAR
    counts = (3, 6, 24, 24, 32, CHUNKS * 3, CHUNKS * 32, CHUNKS * 3)
    bf16 = jnp.bfloat16
    product = pl.pallas_call(
        kernel,
        out_shape=pltpu.VMEM((256, right.shape[1]), bf16),
        in_specs=[pl.BlockSpec(memory_space=pl.ANY)] * 2,
        out_specs=pl.BlockSpec(memory_space=pltpu.VMEM),
        scratch_shapes=[
            pltpu.VMEM((4, 2, 16, depth), bf16),
            pltpu.VMEM((2, 16, depth), bf16),
            pltpu.VMEM((4, 4, 2, 2, 4, 16, depth), bf16),
            *[pltpu.VMEM((4, strip, width), bf16) for width in WIDTHS],
            *[pltpu.VMEM((16, 2, strip * 2, width), bf16) for width in WIDTHS],
            *[pltpu.VMEM((1024, width), jnp.float32) for width in WIDTHS],
            *[pltpu.VMEM((4, 256, width), bf16) for width in WIDTHS * 2],
            regular((5,)),
            regular((5,)),
            dma((2 + 2 * CHUNKS,)),
            *[dma((n,)) for n in counts for _ in range(2)],
        ],
        compiler_params=pltpu.CompilerParams(
            collective_id=0, has_side_effects=True, vmem_limit_bytes=56 * 2**20
        ),
    )(left, right)
    return product.astype(jnp.float32)


def solution(mesh):
    in_specs = (P(("ma", "an"), "ka", None), P("ka", "ma", "an"))
    out_specs = P(("ma", "ka"), "an")
    return jax.shard_map(per_device, mesh=mesh, in_specs=in_specs, out_specs=out_specs, check_vma=False)
```

```python
import jax
import jax.numpy as jnp
from jax import lax
from jax.experimental import pallas as pl
from jax.experimental.pallas import tpu as pltpu
from jax.sharding import PartitionSpec as P

MESH = pl.DeviceIdType.MESH
WIDTHS = (256, 256)
STARTS = tuple(sum(WIDTHS[:ch]) for ch in range(len(WIDTHS)))
QUARTER = sum(WIDTHS)
CHUNKS = len(WIDTHS)


def kernel(left, right, out, hop, relay, rows, *refs):
    refs = list(refs)

    def take_refs(n):
        taken, refs[:n] = refs[:n], []
        return taken

    stage, cols, total, give, take = (take_refs(CHUNKS) for _ in range(5))
    up, down, local, xs_s, xs_r, zm_s, zm_r, p1_s, p1_r, p2_s, p2_r, co_s, co_r, ra_s, ra_r, ri_s, ri_r, ou_s, ou_r = refs
    depth = rows.shape[-1]
    ma, an, hi = lax.axis_index("ma"), lax.axis_index("an"), lax.axis_index("ka")
    lo, y = ma // 4, lax.rem(ma, 4)
    x, c = an // 2, lax.rem(an, 2)
    z = hi * 4 + lo

    def turn(i, d, n=4):
        return lax.rem(i + d + n, n)

    def to_x(d):
        return {"an": turn(x, d) * 2 + c}

    def to_y(d):
        return {"ma": lo * 4 + turn(y, d)}

    def to_z(d):
        level = turn(z, d, 16)
        return {"ma": lax.rem(level, 4) * 4 + y, "ka": level // 4}

    def to_hi(d):
        return {"ka": turn(hi, d)}

    to_core = {"an": x * 2 + 1 - c}

    def remote(src, dst, send, recv, device):
        return pltpu.make_async_remote_copy(
            src_ref=src, dst_ref=dst, send_sem=send, recv_sem=recv, device_id=device, device_id_type=MESH
        )

    barrier = pltpu.get_barrier_semaphore()
    friends = [to(d) for to in (to_x, to_y) for d in (1, 2, 3)] + [to_z(-1), to_core]
    for friend in friends:
        pl.semaphore_signal(barrier, inc=1, device_id=friend, device_id_type=MESH)
    pl.semaphore_wait(barrier, len(friends))

    sent = []

    def send(*args):
        copy = remote(*args)
        copy.start()
        sent.append(copy)

    def flush(keep):
        while len(sent) > keep:
            sent.pop(0).wait_send()

    def await_into(dst, sem):
        remote(dst, dst, sem, sem, to_core).wait_recv()

    def hear(r):
        if r >= 2:
            pl.semaphore_wait(down.at[r - 1], 1)
        if r >= 3:
            pl.semaphore_wait(up.at[r - 1], 1)
        if r <= 4:
            pl.semaphore_signal(down.at[r], inc=1, device_id=to_z(1), device_id_type=MESH)
        if 2 <= r <= 4:
            pl.semaphore_signal(up.at[r], inc=1, device_id=to_z(-1), device_id_type=MESH)

    own = {}

    def start_local(src, dst, i):
        own[i] = pltpu.make_async_copy(src, dst, local.at[i])
        own[i].start()

    def columns(ch, of):
        return pl.ds(pl.multiple_of(of * QUARTER + STARTS[ch], 128), WIDTHS[ch])

    def scatter():
        for d in (2, 1, 3):
            send(left.at[:, turn(x, d)], hop.at[x], xs_s.at[d - 1], xs_r.at[d - 1], to_x(d))
        start_local(left.at[:, x], hop.at[x], 0)

    def spread(ch):
        for d in (2, 1, 3):
            i = ch * 3 + d - 1
            send(right.at[:, columns(ch, turn(y, d))], stage[ch].at[y], ra_s.at[i], ra_r.at[i], to_y(d))
        start_local(right.at[:, columns(ch, y)], stage[ch].at[y], 2 + ch)

    def settle(ch):
        own[2 + ch].wait()
        for d in (1, 2, 3):
            await_into(stage[ch].at[turn(y, -d)], ra_r.at[ch * 3 + d - 1])
        block = stage[ch][...].astype(jnp.float32).reshape(-1, WIDTHS[ch])
        cols[ch][z] = block.astype(jnp.bfloat16).reshape(cols[ch].shape[1:])

    def scattered():
        own[0].wait()
        for d in (1, 2, 3):
            await_into(hop.at[turn(x, -d)], xs_r.at[d - 1])
        start_local(hop.at[hi], rows.at[hi, y, c, :, x], 1)

    def lift(d):
        if d == 2:
            for half, way in ((0, 1), (1, 3)):
                send(hop.at[turn(hi, 2), half], relay.at[half], zm_s.at[half], zm_r.at[half], to_hi(way))
        else:
            send(hop.at[turn(hi, d)], rows.at[hi, y, c, :, x], zm_s.at[1 + d], zm_r.at[1 + d], to_hi(d))

    def lift_on():
        for half, way in ((0, 1), (1, 3)):
            await_into(relay.at[half], zm_r.at[half])
            i = 3 + 2 * half
            send(relay.at[half], rows.at[turn(hi, -way), y, c, half, x], zm_s.at[i], zm_r.at[i], to_hi(way))

    def ring_index(ch, s, way, sub):
        return ((ch * 8 + s - 1) * 2 + way) * 2 + sub

    def ring(ch, s):
        for sub in (0, 1):
            for way in (0, 1):
                sign = 1 - 2 * way
                block = cols[ch].at[turn(z, -sign * (s - 1), 16), sub]
                if s > 1:
                    await_into(block, ri_r.at[ring_index(ch, s - 1, way, sub)])
                if s == 8 and sub != way:
                    continue
                i = ring_index(ch, s, way, sub)
                send(block, block, ri_s.at[i], ri_r.at[i], to_z(sign))

    def ring_end(ch):
        for way in (0, 1):
            await_into(cols[ch].at[turn(z, 8, 16), way], ri_r.at[ring_index(ch, 8, way, way)])

    def gather_one(k):
        block = turn(hi, k)
        if k == 0:
            own[1].wait()
        else:
            if k == 2:
                for half in (0, 1):
                    await_into(rows.at[block, y, c, half, x], zm_r.at[3 + 2 * half])
            else:
                await_into(rows.at[block, y, c, :, x], zm_r.at[5 - k])
        for d in (2, 1, 3):
            i = (k * 3 + d - 1) * 2
            for half, to in ((0, to_x(d)), (1, to_y(d))):
                mine = rows.at[block, y, c, half, x]
                send(mine, mine, p1_s.at[i + half], p1_r.at[i + half], to)

    def gather_two(k):
        block = turn(hi, k)
        for d in (1, 3, 2):
            i = (k * 3 + d - 1) * 2
            await_into(rows.at[block, y, c, 0, turn(x, -d)], p1_r.at[i])
            await_into(rows.at[block, turn(y, -d), c, 1, x], p1_r.at[i + 1])
        for d in (2, 1, 3, 0):
            for half, mine in ((0, rows.at[block, y, c, 0]), (1, rows.at[block, :, c, 1, x])):
                if d == 0:
                    i = k * 8 + half
                    send(mine, mine, co_s.at[i], co_r.at[i], to_core)
                else:
                    i = (k * 3 + d - 1) * 2 + half
                    send(mine, mine, p2_s.at[i], p2_r.at[i], to_x(d) if half else to_y(d))

    def pass_on(k):
        block = turn(hi, k)
        for d in (1, 3, 2):
            i, j = (k * 3 + d - 1) * 2, k * 8 + 2 * d
            for half, got in ((0, rows.at[block, turn(y, -d), c, 0]), (1, rows.at[block, :, c, 1, turn(x, -d)])):
                await_into(got, p2_r.at[i + half])
                send(got, got, co_s.at[j + half], co_r.at[j + half], to_core)

    def get_rest(k):
        block = turn(hi, k)
        for d in (0, 1, 3, 2):
            j = k * 8 + 2 * d
            await_into(rows.at[block, turn(y, -d), 1 - c, 0], co_r.at[j])
            await_into(rows.at[block, :, 1 - c, 1, turn(x, -d)], co_r.at[j + 1])

    begun = set()

    def multiply(ch, k):
        block, first = turn(hi, k), ch not in begun
        begun.add(ch)

        def half(i, carry):
            at = pl.ds(pl.multiple_of(i * 512, 512), 512)
            a = rows[block, pl.ds(i * 2, 2)].reshape(512, depth)
            b = cols[ch][pl.ds(block * 4, 4)].reshape(depth, WIDTHS[ch])
            term = jnp.dot(a, b, preferred_element_type=jnp.float32)
            total[ch][at] = term if first else total[ch][at] + term
            return carry

        lax.fori_loop(0, 2, half, 0)

    def hand_out(ch, k):
        block = turn(hi, k)
        for d in (2, 1, 3, 0):
            of = turn(y, d)
            at = pl.ds(pl.multiple_of(of * 256, 256), 256)
            a = rows[block, of].reshape(256, depth)
            b = cols[ch][pl.ds(block * 4, 4)].reshape(depth, WIDTHS[ch])
            term = jnp.dot(a, b, preferred_element_type=jnp.float32)
            give[ch][of] = (total[ch][at] + term).astype(jnp.bfloat16)
            if d:
                i = ch * 3 + d - 1
                send(give[ch].at[of], take[ch].at[y], ou_s.at[i], ou_r.at[i], to_y(d))
        start_local(give[ch].at[y], take[ch].at[y], 2 + CHUNKS + ch)

    def collect(ch):
        own[2 + CHUNKS + ch].wait()
        for d in (1, 2, 3):
            await_into(take[ch].at[turn(y, -d)], ou_r.at[ch * 3 + d - 1])
        for i in range(4):
            out[:, pl.ds(i * QUARTER + STARTS[ch], WIDTHS[ch])] = take[ch][i]

    hear(1)
    spread(0)
    scatter()
    hear(2)
    settle(0)
    ring(0, 1)
    spread(1)
    hear(3)
    scattered()
    hear(4)
    gather_one(0)
    hear(5)
    lift(1)
    lift(3)
    lift(2)
    settle(1)
    ring(0, 2)
    gather_two(0)
    ring(0, 3)
    ring(1, 1)
    ring(0, 4)
    ring(1, 2)
    lift_on()
    gather_one(1)
    gather_one(3)
    pass_on(0)
    ring(0, 5)
    gather_two(1)
    gather_two(3)
    ring(1, 3)
    gather_one(2)
    ring(0, 6)
    get_rest(0)
    ring(1, 4)
    multiply(0, 0)
    gather_two(2)
    ring(0, 7)
    pass_on(1)
    pass_on(3)
    ring(1, 5)
    get_rest(1)
    get_rest(3)
    ring(0, 8)
    multiply(1, 0)
    multiply(0, 1)
    pass_on(2)
    ring(1, 6)
    multiply(0, 3)
    get_rest(2)
    ring_end(0)
    hand_out(0, 2)
    ring(1, 7)
    ring(1, 8)
    multiply(1, 1)
    collect(0)
    multiply(1, 3)
    ring_end(1)
    hand_out(1, 2)
    flush(3)
    collect(1)
    flush(0)


def per_device(left_matrix, right_matrix):
    depth, strip = left_matrix.shape[2], right_matrix.shape[1]
    left = left_matrix.reshape(2, 4, 16, depth)
    right = right_matrix.reshape(right_matrix.shape[1:])
    dma, regular = pltpu.SemaphoreType.DMA, pltpu.SemaphoreType.REGULAR
    counts = (3, 6, 24, 24, 32, CHUNKS * 3, CHUNKS * 32, CHUNKS * 3)
    bf16 = jnp.bfloat16
    product = pl.pallas_call(
        kernel,
        out_shape=pltpu.VMEM((256, right.shape[1]), bf16),
        in_specs=[pl.BlockSpec(memory_space=pl.ANY)] * 2,
        out_specs=pl.BlockSpec(memory_space=pltpu.VMEM),
        scratch_shapes=[
            pltpu.VMEM((4, 2, 16, depth), bf16),
            pltpu.VMEM((2, 16, depth), bf16),
            pltpu.VMEM((4, 4, 2, 2, 4, 16, depth), bf16),
            *[pltpu.VMEM((4, strip, width), bf16) for width in WIDTHS],
            *[pltpu.VMEM((16, 2, strip * 2, width), bf16) for width in WIDTHS],
            *[pltpu.VMEM((1024, width), jnp.float32) for width in WIDTHS],
            *[pltpu.VMEM((4, 256, width), bf16) for width in WIDTHS * 2],
            regular((5,)),
            regular((5,)),
            dma((2 + 2 * CHUNKS,)),
            *[dma((n,)) for n in counts for _ in range(2)],
        ],
        compiler_params=pltpu.CompilerParams(
            collective_id=0, has_side_effects=True, vmem_limit_bytes=56 * 2**20
        ),
    )(left, right)
    return product.astype(jnp.float32)


def solution(mesh):
    in_specs = (P(("ma", "an"), "ka", None), P("ka", "ma", "an"))
    out_specs = P(("ma", "ka"), "an")
    return jax.shard_map(per_device, mesh=mesh, in_specs=in_specs, out_specs=out_specs, check_vma=False)
```
